256 devices in a mesh: section: 32 (over z_hi, y, core), dp: 8 (over z_lo, x).
Axes of the slice: x: 4, y: 4, z: 8 (z_hi: 4, z_lo: 2; z = z_hi * 2 + z_lo), core: 2. Of those that a mesh axis runs over, the one named last changes fastest.
Arguments:
- activations: bfloat16 [32, 2048, 3072], P('section', 'dp')
- cotangents: bfloat16 [32, 2048, 3072], P('section', 'dp')
- weights: bfloat16 [32, 3072, 3072], P('section', 'dp'), may hold values from -0.109375 to 0.109375
Outputs:
- update: bfloat16 [32, 3072, 3072], P('section', 'dp')
- handed: bfloat16 [32, 2048, 3072], P('section', 'dp')
The draws below stay inside these ranges and needn't reach their ends.
All inputs are finite; a program needn't handle non-finite values.
Results may differ from the reference program's by a relative error of at most 0.017.
Values may be sent and summed in bfloat16 or wider, within the bound.
No kernel may reach another device: no remote copies, remote signals or barrier semaphores. Data moves between devices by JAX's collectives and lax.ppermute only.
A program may use at most 128 MiB of HBM per device.

```python
import math
import jax
import jax.numpy as jnp
import numpy as np
from jax import lax

F = 3072
BLOCK = 384
TOKENS = 2048
LAYERS = 32
N_DP = 8


latent_levels = np.array([int(65536.0 * 2.0 ** (-k / 16.0)) for k in range(128)], dtype=np.float32)


latent_power = float(np.sum((latent_levels / 65536.0) ** 2))


latent_gain = 1.2


noise_gain = 0.2


def spread(key, shape, low, high):
    return jnp.exp(jax.random.uniform(key, shape, jnp.float32, math.log(low), math.log(high)))


def mixture(key, noise, mean_gain, row_low, row_high):
    subkeys = jax.random.split(key, 5)
    count = latent_levels.shape[0]
    token_signs = jnp.where(jax.random.bernoulli(subkeys[0], 0.5, (LAYERS, TOKENS, count)), 1.0, -1.0).astype(jnp.float32)
    load_signs = jnp.where(jax.random.bernoulli(subkeys[1], 0.5, (LAYERS, count, F)), 1.0, -1.0).astype(jnp.float32)
    loadings = load_signs * jnp.asarray(latent_levels)[None, :, None]
    latent = jnp.einsum('ltk,lkf->ltf', token_signs, loadings, precision=lax.Precision.HIGHEST) / 65536.0
    shared = mean_gain * jax.random.normal(subkeys[2], (LAYERS, 1, F), jnp.float32)
    total = mean_gain * mean_gain + latent_gain * latent_gain * latent_power + noise_gain * noise_gain
    unit = (shared + latent_gain * latent + noise_gain * noise) / math.sqrt(total)
    row_scale = spread(subkeys[3], (LAYERS, TOKENS, 1), row_low, row_high)
    col_scale = spread(subkeys[4], (LAYERS, 1, F), 0.5, 5.0)
    return (unit * row_scale * col_scale).astype(jnp.bfloat16)


def draw_activations(key, part):
    key = jax.random.fold_in(key, 1)
    noise_key = jax.random.fold_in(key, 7)
    noise = jnp.clip(jax.random.normal(noise_key, (LAYERS, TOKENS, F), jnp.float32), -6.0, 6.0)
    return mixture(key, noise, 3.0, 0.5, 5.0)


def draw_cotangents(key, part):
    key = jax.random.fold_in(key, 2)
    noise_key = jax.random.fold_in(key, 7)
    noise = jnp.clip(jax.random.normal(noise_key, (LAYERS, TOKENS, F), jnp.float32), -6.0, 6.0)
    return mixture(key, noise, 3.0, 0.5, 5.0)


def block_levels(rng, extent, pieces, least, largest):
    factor_of = 1.0
    for position, parts in pieces:
        heights = jax.random.uniform(jax.random.fold_in(jax.random.fold_in(rng, 6), position), (parts,), jnp.float32, least / len(pieces), largest / len(pieces))
        factor_of = factor_of * jnp.repeat(jnp.exp(heights), extent[position] // parts).reshape((-1,) + (1,) * (len(extent) - 1 - position))
    return factor_of


def bell_draw(stream_key, dims, deviation, bound, shards=(), kind=jnp.bfloat16):
    entries = deviation * jax.random.normal(stream_key, dims, jnp.float32)
    if shards:
        entries = entries * block_levels(stream_key, dims, shards, -0.22, 0.18)
    return jnp.clip(entries, -bound, bound).astype(kind)


def setup_inputs(seed: int = 0) -> dict:
    key_list = jax.random.split(jax.random.key(seed), 4)
    activations = draw_activations(jax.random.fold_in(key_list[3], 71), 0)
    cotangents = draw_cotangents(jax.random.fold_in(key_list[3], 71), 0)
    weights = bell_draw(key_list[2], (LAYERS, F, F), F ** -0.5, 0.109375, ((0, 32), (1, 8)))
    return {"activations": activations, "cotangents": cotangents, "weights": weights}


DAMP = 0.1

def damped(moment, total_rows):
    moment = moment / total_rows
    block_size = moment.shape[0]
    shift_value = DAMP * jnp.trace(moment) / block_size
    return moment + shift_value * jnp.eye(block_size, dtype=jnp.float32)

def factor_solve(matrix, right_side):
    lower = jnp.linalg.cholesky(matrix)
    middle = lax.linalg.triangular_solve(lower, right_side, left_side=True, lower=True)
    return lax.linalg.triangular_solve(lower, middle, left_side=True, lower=True, transpose_a=True)

def precondition(values, total_rows):
    wide = values.astype(jnp.float32).reshape(total_rows, N_DP, BLOCK)
    moments = jnp.einsum('tpb,tpc->pbc', wide, wide, precision=lax.Precision.HIGHEST)
    columns = jnp.transpose(wide, (1, 2, 0))
    solved = jax.vmap(lambda moment, side: factor_solve(damped(moment, total_rows), side))(moments, columns)
    return solved.astype(jnp.bfloat16).reshape(N_DP * BLOCK, total_rows)

def one_layer(operands):
    act_tok, cot_tok, weight_rows = operands
    total_rows = act_tok.shape[0]
    act_hat = precondition(act_tok, total_rows)
    cot_hat = precondition(cot_tok, total_rows)
    product = lax.dot_general(cot_hat.astype(jnp.float32), act_hat.astype(jnp.float32), (((1,), (1,)), ((), ())), preferred_element_type=jnp.float32)
    update = (product / total_rows).astype(jnp.bfloat16)

    def add_block(running, index):
        cot_block = lax.dynamic_slice_in_dim(cot_tok, index * BLOCK, BLOCK, 1)
        weight_block = lax.dynamic_slice_in_dim(weight_rows, index * BLOCK, BLOCK, 0)
        term = jnp.dot(cot_block.astype(jnp.float32), weight_block.astype(jnp.float32), preferred_element_type=jnp.float32).astype(jnp.bfloat16)
        term = lax.optimization_barrier(term)
        return (running + term.astype(jnp.float32), None)
    start_sum = jnp.zeros((total_rows, weight_rows.shape[1]), jnp.float32)
    back, unused = lax.scan(add_block, start_sum, jnp.arange(N_DP, dtype=jnp.int32))
    return (update, back.astype(jnp.bfloat16))

def reference(activations, cotangents, weights):
    update, back = lax.map(one_layer, (activations, cotangents, weights))
    zero_rows = jnp.zeros((1, back.shape[1], back.shape[2]), jnp.bfloat16)
    handed = jnp.concatenate([back[1:], zero_rows], axis=0)
    return (update, handed)
```

```python
import functools

import jax
import jax.numpy as jnp
from jax import lax
from jax.experimental import pallas as pl
from jax.experimental.pallas import tpu as pltpu
from jax.sharding import PartitionSpec as P

DAMP = 0.1
TILE = 128
GROUP = 8
RING = 4
MIB = 1024 * 1024


def terms(value):
    first = value.astype(jnp.bfloat16)
    rest = value - first.astype(jnp.float32)
    second = rest.astype(jnp.bfloat16)
    third = (rest - second.astype(jnp.float32)).astype(jnp.bfloat16)
    return first, second, third


def dot_wide(left, right):
    a, b, c = terms(left)
    x, y, z = terms(right)
    return jnp.dot(
        jnp.concatenate([a, a, a, b, b, c], axis=1),
        jnp.concatenate([x, y, z, x, y, x], axis=0),
        preferred_element_type=jnp.float32,
    )


def pivot_group(matrix):
    count, size = matrix.shape[0], matrix.shape[1]
    lane = lax.broadcasted_iota(jnp.int32, (count, GROUP, size), 2)
    row = lax.broadcasted_iota(jnp.int32, (count, GROUP, size), 1)
    columns = [jnp.broadcast_to(matrix[:, :, s : s + 1], (count, size, size)) for s in range(GROUP)]
    head = matrix[:, :GROUP]
    near = [column[:, :GROUP] for column in columns]
    for t in range(GROUP):
        inverse = 1.0 / near[t][:, t : t + 1]
        pivot_row = jnp.where(lane[:, :1] == t, inverse, head[:, t : t + 1] * inverse)
        head = jnp.where(row == t, pivot_row, jnp.where(lane == t, 0.0, head) - near[t] * pivot_row)
        for s in range(t + 1, GROUP):
            scaled = near[s][:, t : t + 1] * inverse
            near[s] = jnp.where(row == t, scaled, near[s] - near[t] * scaled)
    wide_lane = lax.broadcasted_iota(jnp.int32, (count, size - GROUP, size), 2)
    rest = jnp.where(wide_lane < GROUP, 0.0, matrix[:, GROUP:])
    for s in range(GROUP):
        rest = rest - columns[s][:, GROUP:] * head[:, s : s + 1]
    turned = jnp.concatenate([rest, head], axis=1)
    return pltpu.roll(turned, size - GROUP, 2)


def white_kernel(starts, block, total_rows, flipped, rows_of, *refs):
    pieces = refs[: len(rows_of)]
    out_ref, whole, tile, stacked = refs[len(rows_of) :]
    count = len(starts)
    eye = lax.broadcasted_iota(jnp.int32, (block, block), 0) == lax.broadcasted_iota(
        jnp.int32, (block, block), 1
    )
    for m in range(count):
        moment = jnp.zeros((block, block), jnp.float32)
        for piece in pieces:
            part = piece[:, starts[m] : starts[m] + block]
            moment += lax.dot_general(part, part, (((0,), (0,)), ((), ())), preferred_element_type=jnp.float32)
        moment = moment / total_rows
        shift = DAMP * jnp.sum(jnp.where(eye, moment, 0.0)) / block
        whole[m] = moment + jnp.where(eye, shift, 0.0)
    steps = block // TILE
    for k in range(steps):
        mine = slice(k * TILE, (k + 1) * TILE)
        others = [slice(j * TILE, (j + 1) * TILE) for j in range(steps) if j != k]
        for m in range(count):
            tile[m] = whole[m, mine, mine]

        def turn(step, carry):
            tile[...] = pivot_group(tile[...])
            return carry

        lax.fori_loop(0, TILE // GROUP, turn, 0)
        for m in range(count):
            pivot = tile[m]
            across = jnp.concatenate([whole[m, mine, j] for j in others], axis=1)
            down = jnp.concatenate([whole[m, i, mine] for i in others], axis=0)
            solved = dot_wide(pivot, across)
            left = dot_wide(down, pivot)
            change = dot_wide(down, solved)
            whole[m, mine, mine] = pivot
            for a, i in enumerate(others):
                here = slice(a * TILE, (a + 1) * TILE)
                whole[m, mine, i] = solved[:, here]
                whole[m, i, mine] = -left[here]
                for b, j in enumerate(others):
                    whole[m, i, j] = whole[m, i, j] - change[here, b * TILE : (b + 1) * TILE]
    for m in range(count):
        for t, term in enumerate(terms(whole[m])):
            stacked[m, t * block : (t + 1) * block] = term

    def apply(m, carry):
        lanes = pl.ds(pl.multiple_of(m * block, TILE), block)
        for piece, places in zip(pieces, rows_of):
            for first, length, place in places:
                part = piece[first : first + length, lanes]
                wide = jnp.concatenate([part, part, part], axis=1)
                if flipped:
                    value = lax.dot_general(
                        stacked[m], wide, (((0,), (1,)), ((), ())), preferred_element_type=jnp.float32
                    )
                    out_ref[pl.ds(pl.multiple_of(m * block, TILE), block), place : place + length] = value.astype(
                        jnp.bfloat16
                    )
                else:
                    value = jnp.dot(wide, stacked[m], preferred_element_type=jnp.float32)
                    out_ref[place : place + length, lanes] = value.astype(jnp.bfloat16)
        return carry

    lax.fori_loop(0, count, apply, 0)


def whitened(pieces, rows_of, block, flipped):
    width = pieces[0].shape[1]
    count = width // block
    rows = sum(piece.shape[0] for piece in pieces)
    starts = tuple(m * block for m in range(count))
    shape = (width, rows) if flipped else (rows, width)
    return pl.pallas_call(
        functools.partial(white_kernel, starts, block, rows, flipped, rows_of),
        out_shape=jax.ShapeDtypeStruct(shape, jnp.bfloat16),
        in_specs=[pl.BlockSpec(memory_space=pltpu.VMEM)] * len(pieces),
        out_specs=pl.BlockSpec(memory_space=pltpu.VMEM),
        scratch_shapes=[
            pltpu.VMEM((count, block, block), jnp.float32),
            pltpu.VMEM((count, TILE, TILE), jnp.float32),
            pltpu.VMEM((count, 3 * block, block), jnp.bfloat16),
        ],
        compiler_params=pltpu.CompilerParams(vmem_limit_bytes=48 * MIB),
        cost_estimate=pl.CostEstimate(
            flops=count * (8 * rows * block * block + 200 * block**3), bytes_accessed=4 * rows * width, transcendentals=0
        ),
        name="whitened",
    )(*pieces)


def along_x(value, steps):
    pairs = [(z * RING + x, z * RING + (x + steps) % RING) for z in range(2) for x in range(RING)]
    return lax.ppermute(value, "dp", pairs)


def across_z(value):
    return lax.ppermute(value, "dp", [(i, (i + RING) % (2 * RING)) for i in range(2 * RING)])


def handed_down(value, cross):
    layers, devices = lax.axis_size("section"), 2 * RING
    shift = RING if cross else 0
    pairs = [
        (layer * devices + i, (layer - 1) * devices + (i + shift) % devices)
        for layer in range(1, layers)
        for i in range(devices)
    ]
    return lax.ppermute(value, ("section", "dp"), pairs)


def tied(value, after):
    return lax.optimization_barrier((value, after))[0]


def joined(z, mine, other, axis):
    return jnp.where(
        z == 0, jnp.concatenate([mine, other], axis=axis), jnp.concatenate([other, mine], axis=axis)
    )


def shards(activations, cotangents, weights):
    act_tok = activations[0]
    cot_tok = cotangents[0]
    weight_rows = weights[0]
    place = lax.axis_index("dp")
    z, x = place // RING, place % RING
    local_rows, features = act_tok.shape
    block = features // (2 * RING)
    half = features // 2

    def columns(value, start, width):
        return lax.dynamic_slice_in_dim(value, start, width, 1)

    act_mine = columns(act_tok, z * half, half)
    act_theirs = across_z(columns(act_tok, (1 - z) * half, half))
    act_own = jnp.concatenate([act_mine, act_theirs], axis=0)
    cot_four = cot_tok.reshape(local_rows, 2, RING, block)

    def cot_for(target):
        return lax.dynamic_slice_in_dim(cot_four, target, 1, 2).reshape(local_rows, 2 * block)

    cot_slots = [cot_for(x)]
    for k in range(1, RING):
        cot_slots.append(along_x(cot_for((x + k) % RING), k))
    cot_here = jnp.concatenate(cot_slots, axis=0)
    cot_there = across_z(cot_here)
    act_slots = [act_own] + [along_x(act_own, k) for k in range(1, RING)]
    weight_theirs = across_z(tied(columns(weight_rows, (1 - z) * half, half), cot_there))
    weight_pair = joined(z, columns(weight_rows, z * half, half), weight_theirs, 0)

    rows_act = tuple(
        ((0, local_rows, k * local_rows), (local_rows, local_rows, (RING + k) * local_rows)) for k in range(RING)
    )
    ring_rows = RING * local_rows
    rows_cot = (((0, ring_rows, 0),), ((0, ring_rows, ring_rows),))
    cot_hat = whitened((cot_here, cot_there), rows_cot, block, True)

    def back_of(tokens):
        part = jnp.dot(tokens, weight_pair, preferred_element_type=jnp.float32).astype(jnp.bfloat16)
        part = part.reshape(RING, local_rows, half)
        total = part[0].astype(jnp.float32)
        for k in range(1, RING):
            total = total + along_x(part[k], -k).astype(jnp.float32)
        return total.astype(jnp.bfloat16)

    back_there = handed_down(back_of(cot_there), True)
    back_here = handed_down(back_of(cot_here), False)
    handed = joined(z, back_here, back_there, 1)

    act_hat = whitened(act_slots, rows_act, block, False)
    total_rows = act_hat.shape[0]

    def update_of(rows):
        product = jnp.dot(rows, act_hat, preferred_element_type=jnp.float32)
        return (product / total_rows).astype(jnp.bfloat16)

    sent = across_z(update_of(lax.dynamic_slice_in_dim(cot_hat, (1 - z) * block, block, 0)))
    kept = update_of(lax.dynamic_slice_in_dim(cot_hat, z * block, block, 0))
    update = joined(z, kept, sent, 1)
    return (update[None], handed[None])


def solution(mesh):
    placed = P("section", "dp", None)
    return jax.shard_map(
        shards,
        mesh=mesh,
        in_specs=(placed, placed, placed),
        out_specs=(placed, placed),
        check_vma=False,
    )
```

```python
import functools

import jax
import jax.numpy as jnp
from jax import lax
from jax.experimental import pallas as pl
from jax.experimental.pallas import tpu as pltpu
from jax.sharding import PartitionSpec as P

DAMP = 0.1
TILE = 128
GROUP = 8
RING = 4
MIB = 1024 * 1024


def terms(value):
    first = value.astype(jnp.bfloat16)
    rest = value - first.astype(jnp.float32)
    second = rest.astype(jnp.bfloat16)
    third = (rest - second.astype(jnp.float32)).astype(jnp.bfloat16)
    return first, second, third


def dot_wide(left, right):
    a, b, c = terms(left)
    x, y, z = terms(right)
    return jnp.dot(
        jnp.concatenate([a, a, a, b, b, c], axis=1),
        jnp.concatenate([x, y, z, x, y, x], axis=0),
        preferred_element_type=jnp.float32,
    )


def panel_rows(head, first):
    near = [jnp.broadcast_to(head[:, :, first + s : first + s + 1], head.shape) for s in range(GROUP)]
    lane = lax.broadcasted_iota(jnp.int32, head.shape, 2)
    row = lax.broadcasted_iota(jnp.int32, head.shape, 1)
    for t in range(GROUP):
        inverse = 1.0 / near[t][:, t : t + 1]
        pivot_row = jnp.where(lane[:, :1] == first + t, inverse, head[:, t : t + 1] * inverse)
        head = jnp.where(row == t, pivot_row, jnp.where(lane == first + t, 0.0, head) - near[t] * pivot_row)
        for s in range(t + 1, GROUP):
            scaled = near[s][:, t : t + 1] * inverse
            near[s] = jnp.where(row == t, scaled, near[s] - near[t] * scaled)
    return head


def applied(rows, after, first):
    width = after.shape[1]
    lane = lax.broadcasted_iota(jnp.int32, rows.shape, 2)
    parts = [
        jnp.broadcast_to(rows[:, :, first + s : first + s + 1], rows.shape) * after[:, s : s + 1] for s in range(width)
    ]
    while len(parts) > 1:
        parts = [p + q for p, q in zip(parts[::2], parts[1::2])]
    return jnp.where((lane >= first) & (lane < first + width), 0.0, rows) - parts[0]


def float_terms(value):
    return [term.astype(jnp.float32) for term in terms(value)]


def rank_update(matrix, before, after, first):
    size, width = matrix.shape[0], before.shape[0]
    lane = lax.broadcasted_iota(jnp.int32, before.shape, 1)
    a, b, c = float_terms(jnp.where(lane < first, -before, before))
    x, y, z = float_terms(after)
    change = lax.dot_general(
        jnp.concatenate([a, a, a, b, b, c], axis=0).astype(jnp.bfloat16),
        jnp.concatenate([x, y, z, x, y, x], axis=0).astype(jnp.bfloat16),
        (((0,), (0,)), ((), ())),
        preferred_element_type=jnp.float32,
    )
    wide_lane = lax.broadcasted_iota(jnp.int32, (size, size), 1)
    kept = jnp.where((wide_lane >= first) & (wide_lane < first + width), 0.0, matrix) - change
    pieces = [kept[:first], after, kept[first + width :]]
    return jnp.concatenate([piece for piece in pieces if piece.shape[0]], axis=0)


def invert_tiles(tile):
    count, size = tile.shape[0], tile.shape[1]
    step = 2 * GROUP
    head = tile[:, :step]
    for first in range(0, size, step):
        top = panel_rows(head[:, :GROUP], first)
        low = panel_rows(applied(head[:, GROUP:], top, first), first + GROUP)
        after = jnp.concatenate([applied(top, low, first + GROUP), low], axis=1)
        before = head
        if first + step < size:
            head = applied(tile[:, first + step : first + 2 * step], after, first)
        for m in range(count):
            tile[m] = rank_update(tile[m], before[m], after[m], first)


def damped_moments(pieces, whole, block, total_rows):
    count = whole.shape[0]
    eye = lax.broadcasted_iota(jnp.int32, (block, block), 0) == lax.broadcasted_iota(
        jnp.int32, (block, block), 1
    )

    def moment_of(m, carry):
        lanes = pl.ds(pl.multiple_of(m * block, TILE), block)
        moment = jnp.zeros((block, block), jnp.float32)
        for piece in pieces:
            part = piece[:, lanes]
            moment += lax.dot_general(part, part, (((0,), (0,)), ((), ())), preferred_element_type=jnp.float32)
        moment = moment / total_rows
        shift = DAMP * jnp.sum(jnp.where(eye, moment, 0.0)) / block
        whole[m] = moment + jnp.where(eye, shift, 0.0)
        return carry

    lax.fori_loop(0, count, moment_of, 0)


def invert_blocks(whole, tile):
    count, block = whole.shape[0], whole.shape[1]
    steps = block // TILE
    for k in range(steps):
        mine = slice(k * TILE, (k + 1) * TILE)
        others = [slice(j * TILE, (j + 1) * TILE) for j in range(steps) if j != k]
        for m in range(count):
            tile[m] = whole[m, mine, mine]
        invert_tiles(tile)
        for m in range(count):
            pivot = tile[m]
            across = jnp.concatenate([whole[m, mine, j] for j in others], axis=1)
            down = jnp.concatenate([whole[m, i, mine] for i in others], axis=0)
            solved = dot_wide(pivot, across)
            left = dot_wide(down, pivot)
            change = dot_wide(down, solved)
            whole[m, mine, mine] = pivot
            for a, i in enumerate(others):
                here = slice(a * TILE, (a + 1) * TILE)
                whole[m, mine, i] = solved[:, here]
                whole[m, i, mine] = -left[here]
                for b, j in enumerate(others):
                    whole[m, i, j] = whole[m, i, j] - change[here, b * TILE : (b + 1) * TILE]


def scratch_for(count, block):
    return [
        pltpu.VMEM((count, block, block), jnp.float32),
        pltpu.VMEM((count, TILE, TILE), jnp.float32),
    ]


def cot_kernel(places, block, total_rows, *refs):
    pieces = refs[: len(places)]
    out_ref, stacked, whole, *work = refs[len(places) :]
    count = whole.shape[0]
    damped_moments(pieces, whole, block, total_rows)
    invert_blocks(whole, *work)
    for m in range(count):
        stacked[m] = jnp.concatenate(terms(whole[m]), axis=0)

    def apply(m, carry):
        lanes = pl.ds(pl.multiple_of(m * block, TILE), block)
        for piece, spots in zip(pieces, places):
            for first, length, place in spots:
                part = piece[first : first + length, lanes]
                value = lax.dot_general(
                    stacked[m],
                    jnp.concatenate([part, part, part], axis=1),
                    (((0,), (1,)), ((), ())),
                    preferred_element_type=jnp.float32,
                )
                out_ref[lanes, place : place + length] = value.astype(jnp.bfloat16)
        return carry

    lax.fori_loop(0, count, apply, 0)


def cot_whitened(pieces, places, block):
    width = pieces[0].shape[1]
    count = width // block
    rows = sum(piece.shape[0] for piece in pieces)
    return pl.pallas_call(
        functools.partial(cot_kernel, places, block, rows),
        out_shape=jax.ShapeDtypeStruct((width, rows), jnp.bfloat16),
        in_specs=[pl.BlockSpec(memory_space=pltpu.VMEM)] * len(pieces),
        out_specs=pl.BlockSpec(memory_space=pltpu.VMEM),
        scratch_shapes=[pltpu.VMEM((count, 3 * block, block), jnp.bfloat16)] + scratch_for(count, block),
        compiler_params=pltpu.CompilerParams(vmem_limit_bytes=48 * MIB),
        cost_estimate=pl.CostEstimate(
            flops=30 * 10**9, bytes_accessed=4 * rows * width, transcendentals=0
        ),
        name="cot_whitened",
    )(*pieces)


def act_kernel(block, total_rows, *refs):
    pieces = refs[:-3]
    out_ref, whole, *work = refs[-3:]
    damped_moments(pieces, whole, block, total_rows)
    invert_blocks(whole, *work)
    for m in range(whole.shape[0]):
        out_ref[m] = jnp.concatenate(terms(whole[m]), axis=0)


def act_inverses(pieces, block):
    width = pieces[0].shape[1]
    count = width // block
    rows = sum(piece.shape[0] for piece in pieces)
    return pl.pallas_call(
        functools.partial(act_kernel, block, rows),
        out_shape=jax.ShapeDtypeStruct((count, 3 * block, block), jnp.bfloat16),
        in_specs=[pl.BlockSpec(memory_space=pltpu.VMEM)] * len(pieces),
        out_specs=pl.BlockSpec(memory_space=pltpu.VMEM),
        scratch_shapes=scratch_for(count, block),
        compiler_params=pltpu.CompilerParams(vmem_limit_bytes=48 * MIB),
        cost_estimate=pl.CostEstimate(flops=40 * 10**9, bytes_accessed=2 * rows * width, transcendentals=0),
        name="act_inverses",
    )(*pieces)


def update_kernel(total_rows, *refs):
    cot_ref, inverse_ref, *pieces, out_ref, stacked = refs
    count, depth, block = inverse_ref.shape
    depth = depth // 3
    for m in range(count):
        stacked[m, : 3 * depth] = inverse_ref[m]
        stacked[m, 3 * depth : 5 * depth] = inverse_ref[m, : 2 * depth]
        stacked[m, 5 * depth :] = inverse_ref[m, :depth]

    def rows_of(i, carry):
        here = pl.ds(pl.multiple_of(i * TILE, TILE), TILE)
        start = 0
        wide = jnp.zeros((TILE, count * block), jnp.float32)
        for piece in pieces:
            length = piece.shape[0]
            wide += jnp.dot(cot_ref[here, start : start + length], piece[...], preferred_element_type=jnp.float32)
            start += length
        wide = wide / total_rows
        for m in range(count):
            lanes = slice(m * block, (m + 1) * block)
            a, b, c = terms(wide[:, lanes])
            value = jnp.dot(
                jnp.concatenate([a, a, a, b, b, c], axis=1), stacked[m], preferred_element_type=jnp.float32
            )
            out_ref[here, lanes] = value.astype(jnp.bfloat16)
        return carry

    lax.fori_loop(0, cot_ref.shape[0] // TILE, rows_of, 0)


def update_of(cot_hat, inverses, pieces):
    width = pieces[0].shape[1]
    rows, tokens = cot_hat.shape
    count, depth, block = inverses.shape
    return pl.pallas_call(
        functools.partial(update_kernel, tokens),
        out_shape=jax.ShapeDtypeStruct((rows, width), jnp.bfloat16),
        in_specs=[pl.BlockSpec(memory_space=pltpu.VMEM)] * (2 + len(pieces)),
        out_specs=pl.BlockSpec(memory_space=pltpu.VMEM),
        scratch_shapes=[pltpu.VMEM((count, 2 * depth, block), jnp.bfloat16)],
        compiler_params=pltpu.CompilerParams(vmem_limit_bytes=48 * MIB),
        cost_estimate=pl.CostEstimate(flops=12 * 10**9, bytes_accessed=2 * tokens * width, transcendentals=0),
        name="update_tiles",
    )(cot_hat, inverses, *pieces)


def along_x(value, steps):
    pairs = [(z * RING + x, z * RING + (x + steps) % RING) for z in range(2) for x in range(RING)]
    return lax.ppermute(value, "dp", pairs)


def across_z(value):
    return lax.ppermute(value, "dp", [(i, (i + RING) % (2 * RING)) for i in range(2 * RING)])


def handed_down(value, cross):
    layers, devices = lax.axis_size("section"), 2 * RING
    shift = RING if cross else 0
    pairs = [
        (layer * devices + i, (layer - 1) * devices + (i + shift) % devices)
        for layer in range(1, layers)
        for i in range(devices)
    ]
    return lax.ppermute(value, ("section", "dp"), pairs)


def tied(value, after):
    return lax.optimization_barrier((value, after))[0]


def joined(z, mine, other, axis):
    return jnp.where(
        z == 0, jnp.concatenate([mine, other], axis=axis), jnp.concatenate([other, mine], axis=axis)
    )


def shards(activations, cotangents, weights):
    act_tok = activations[0]
    cot_tok = cotangents[0]
    weight_rows = weights[0]
    place = lax.axis_index("dp")
    z, x = place // RING, place % RING
    local_rows, features = act_tok.shape
    block = features // (2 * RING)
    half = features // 2

    def columns(value, start, width):
        return lax.dynamic_slice_in_dim(value, start, width, 1)

    act_theirs = across_z(columns(act_tok, (1 - z) * half, half))

    def cot_for(target):
        return jnp.concatenate(
            [columns(cot_tok, target * block, block), columns(cot_tok, (target + RING) * block, block)], axis=1
        )

    cot_slots = [along_x(cot_for((x + k) % RING), k) for k in range(1, RING)]
    act_theirs, *cot_slots = lax.optimization_barrier((act_theirs, *cot_slots))
    act_own = jnp.concatenate([columns(act_tok, z * half, half), act_theirs], axis=0)
    act_slots = [act_own] + [along_x(act_own, k) for k in range(1, RING)]
    cot_here = jnp.concatenate([cot_for(x)] + cot_slots, axis=0)
    cot_there = across_z(cot_here)
    weight_theirs = across_z(tied(columns(weight_rows, (1 - z) * half, half), cot_there))
    weight_pair = joined(z, columns(weight_rows, z * half, half), weight_theirs, 0)

    places = tuple(
        tuple((k * local_rows, local_rows, (2 * k + other) * local_rows) for k in range(RING)) for other in range(2)
    )
    cot_hat = cot_whitened((cot_here, cot_there), places, block)

    def parts_of(tokens):
        part = jnp.dot(tokens, weight_pair, preferred_element_type=jnp.float32).astype(jnp.bfloat16)
        return part.reshape(RING, local_rows, half)

    def summed(part, moved):
        total = part[0].astype(jnp.float32)
        for value in moved:
            total = total + value.astype(jnp.float32)
        return total.astype(jnp.bfloat16)

    parts_there, parts_here = parts_of(cot_there), parts_of(cot_here)
    cot_hat, parts_there, parts_here = lax.optimization_barrier((cot_hat, parts_there, parts_here))
    moved_there = [along_x(parts_there[k], -k) for k in (2, 1, 3)]
    moved_here = [along_x(parts_here[k], -k) for k in (1, 3)]
    inverses = act_inverses(act_slots, block)
    inverses, parts_far, *moved_there = lax.optimization_barrier((inverses, parts_here[2], *moved_there))
    moved_here.append(along_x(parts_far, -2))
    sum_there = summed(parts_there, moved_there)
    back_there = handed_down(sum_there, True)
    tiles = update_of(cot_hat, tied(inverses, sum_there), act_slots)
    back_here = handed_down(summed(parts_here, moved_here), False)
    handed = joined(z, back_here, back_there, 1)

    tiles, back_there = lax.optimization_barrier((tiles, back_there))
    sent = across_z(lax.dynamic_slice_in_dim(tiles, (1 - z) * block, block, 0))
    update = joined(z, lax.dynamic_slice_in_dim(tiles, z * block, block, 0), sent, 1)
    return (update[None], handed[None])


def solution(mesh):
    placed = P("section", "dp", None)
    return jax.shard_map(
        shards,
        mesh=mesh,
        in_specs=(placed, placed, placed),
        out_specs=(placed, placed),
        check_vma=False,
    )
```

```python
import functools

import jax
import jax.numpy as jnp
from jax import lax
from jax.experimental import pallas as pl
from jax.experimental.pallas import tpu as pltpu
from jax.sharding import PartitionSpec as P

DAMP = 0.1
TILE = 128
GROUP = 8
RING = 4
PLANE = 8
MIB = 1024 * 1024


def terms(value):
    first = value.astype(jnp.bfloat16)
    rest = value - first.astype(jnp.float32)
    second = rest.astype(jnp.bfloat16)
    third = (rest - second.astype(jnp.float32)).astype(jnp.bfloat16)
    return first, second, third


def dot_wide(left, right):
    a, b, c = terms(left)
    x, y, z = terms(right)
    return jnp.dot(
        jnp.concatenate([a, a, a, b, b, c], axis=1),
        jnp.concatenate([x, y, z, x, y, x], axis=0),
        preferred_element_type=jnp.float32,
    )


def panel_rows(head, first):
    near = [jnp.broadcast_to(head[:, :, first + s : first + s + 1], head.shape) for s in range(GROUP)]
    lane = lax.broadcasted_iota(jnp.int32, head.shape, 2)
    row = lax.broadcasted_iota(jnp.int32, head.shape, 1)
    for t in range(GROUP):
        inverse = 1.0 / near[t][:, t : t + 1]
        pivot_row = jnp.where(lane[:, :1] == first + t, inverse, head[:, t : t + 1] * inverse)
        head = jnp.where(row == t, pivot_row, jnp.where(lane == first + t, 0.0, head) - near[t] * pivot_row)
        for s in range(t + 1, GROUP):
            scaled = near[s][:, t : t + 1] * inverse
            near[s] = jnp.where(row == t, scaled, near[s] - near[t] * scaled)
    return head


def applied(rows, after, first):
    width = after.shape[1]
    lane = lax.broadcasted_iota(jnp.int32, rows.shape, 2)
    parts = [
        jnp.broadcast_to(rows[:, :, first + s : first + s + 1], rows.shape) * after[:, s : s + 1] for s in range(width)
    ]
    while len(parts) > 1:
        parts = [p + q for p, q in zip(parts[::2], parts[1::2])]
    return jnp.where((lane >= first) & (lane < first + width), 0.0, rows) - parts[0]


def float_terms(value):
    return [term.astype(jnp.float32) for term in terms(value)]


def rank_update(matrix, before, after, first):
    size, width = matrix.shape[0], before.shape[0]
    lane = lax.broadcasted_iota(jnp.int32, before.shape, 1)
    a, b, c = float_terms(jnp.where(lane < first, -before, before))
    x, y, z = float_terms(after)
    change = lax.dot_general(
        jnp.concatenate([a, a, a, b, b, c], axis=0).astype(jnp.bfloat16),
        jnp.concatenate([x, y, z, x, y, x], axis=0).astype(jnp.bfloat16),
        (((0,), (0,)), ((), ())),
        preferred_element_type=jnp.float32,
    )
    wide_lane = lax.broadcasted_iota(jnp.int32, (size, size), 1)
    kept = jnp.where((wide_lane >= first) & (wide_lane < first + width), 0.0, matrix) - change
    pieces = [kept[:first], after, kept[first + width :]]
    return jnp.concatenate([piece for piece in pieces if piece.shape[0]], axis=0)


def invert_tiles(tile):
    count, size = tile.shape[0], tile.shape[1]
    step = 2 * GROUP
    head = tile[:, :step]
    for first in range(0, size, step):
        top = panel_rows(head[:, :GROUP], first)
        low = panel_rows(applied(head[:, GROUP:], top, first), first + GROUP)
        after = jnp.concatenate([applied(top, low, first + GROUP), low], axis=1)
        before = head
        if first + step < size:
            head = applied(tile[:, first + step : first + 2 * step], after, first)
        for m in range(count):
            tile[m] = rank_update(tile[m], before[m], after[m], first)


def damped_moments(pieces, whole, block, total_rows):
    count = whole.shape[0]
    eye = lax.broadcasted_iota(jnp.int32, (block, block), 0) == lax.broadcasted_iota(
        jnp.int32, (block, block), 1
    )

    def moment_of(m, carry):
        lanes = pl.ds(pl.multiple_of(m * block, TILE), block)
        moment = jnp.zeros((block, block), jnp.float32)
        for piece in pieces:
            part = piece[:, lanes]
            moment += lax.dot_general(part, part, (((0,), (0,)), ((), ())), preferred_element_type=jnp.float32)
        moment = moment / total_rows
        shift = DAMP * jnp.sum(jnp.where(eye, moment, 0.0)) / block
        whole[m] = moment + jnp.where(eye, shift, 0.0)
        return carry

    lax.fori_loop(0, count, moment_of, 0)


def invert_blocks(whole, tile):
    count, block = whole.shape[0], whole.shape[1]
    steps = block // TILE
    for k in range(steps):
        mine = slice(k * TILE, (k + 1) * TILE)
        others = [slice(j * TILE, (j + 1) * TILE) for j in range(steps) if j != k]
        for m in range(count):
            tile[m] = whole[m, mine, mine]
        invert_tiles(tile)
        for m in range(count):
            pivot = tile[m]
            across = jnp.concatenate([whole[m, mine, j] for j in others], axis=1)
            down = jnp.concatenate([whole[m, i, mine] for i in others], axis=0)
            solved = dot_wide(pivot, across)
            left = dot_wide(down, pivot)
            change = dot_wide(down, solved)
            whole[m, mine, mine] = pivot
            for a, i in enumerate(others):
                here = slice(a * TILE, (a + 1) * TILE)
                whole[m, mine, i] = solved[:, here]
                whole[m, i, mine] = -left[here]
                for b, j in enumerate(others):
                    whole[m, i, j] = whole[m, i, j] - change[here, b * TILE : (b + 1) * TILE]


def scratch_for(count, block):
    return [
        pltpu.VMEM((count, block, block), jnp.float32),
        pltpu.VMEM((count, TILE, TILE), jnp.float32),
    ]


def cot_kernel(places, block, total_rows, place_ref, *refs):
    pieces = refs[: len(places)]
    *outs, stacked, whole, tile = refs[len(places) :]
    count = whole.shape[0]
    damped_moments(pieces, whole, block, total_rows)
    invert_blocks(whole, tile)
    for m in range(count):
        stacked[m] = jnp.concatenate(terms(whole[m]), axis=0)
    own = place_ref[0]
    for out_ref, m in zip(outs, (1 - own, own)):
        lanes = pl.ds(pl.multiple_of(m * block, TILE), block)
        for piece, spots in zip(pieces, places):
            for first, length, place in spots:
                part = piece[first : first + length, lanes]
                value = lax.dot_general(
                    stacked[m],
                    jnp.concatenate([part, part, part], axis=1),
                    (((0,), (1,)), ((), ())),
                    preferred_element_type=jnp.float32,
                )
                out_ref[:, place : place + length] = value.astype(jnp.bfloat16)


def cot_whitened(z, pieces, places, block):
    width = pieces[0].shape[1]
    count = width // block
    rows = sum(piece.shape[0] for piece in pieces)
    return pl.pallas_call(
        functools.partial(cot_kernel, places, block, rows),
        out_shape=[jax.ShapeDtypeStruct((block, rows), jnp.bfloat16)] * 2,
        in_specs=[pl.BlockSpec(memory_space=pltpu.SMEM)] + [pl.BlockSpec(memory_space=pltpu.VMEM)] * len(pieces),
        out_specs=[pl.BlockSpec(memory_space=pltpu.VMEM)] * 2,
        scratch_shapes=[pltpu.VMEM((count, 3 * block, block), jnp.bfloat16)] + scratch_for(count, block),
        compiler_params=pltpu.CompilerParams(vmem_limit_bytes=48 * MIB),
        cost_estimate=pl.CostEstimate(flops=30 * 10**9, bytes_accessed=4 * rows * width, transcendentals=0),
        name="cot_whitened",
    )(z[None], *pieces)


def back_kernel(slots, chunk, *refs):
    *pieces, weight_ref = refs[:-slots]
    outs = refs[-slots:]
    rows = outs[0].shape[0]

    def columns_of(i, carry):
        lanes = pl.ds(pl.multiple_of(i * chunk, TILE), chunk)
        weight = weight_ref[:, lanes]
        at = 0
        for piece in pieces:
            value = jnp.dot(piece[...], weight, preferred_element_type=jnp.float32).astype(jnp.bfloat16)
            for first in range(0, piece.shape[0], rows):
                outs[at][:, lanes] = value[first : first + rows]
                at += 1
        return carry

    lax.fori_loop(0, weight_ref.shape[1] // chunk, columns_of, 0)


def back_parts(pieces, weight, rows):
    total = sum(piece.shape[0] for piece in pieces)
    slots = total // rows
    depth, width = weight.shape
    return pl.pallas_call(
        functools.partial(back_kernel, slots, 2 * TILE),
        out_shape=[jax.ShapeDtypeStruct((rows, width), jnp.bfloat16)] * slots,
        in_specs=[pl.BlockSpec(memory_space=pltpu.VMEM)] * (len(pieces) + 1),
        out_specs=[pl.BlockSpec(memory_space=pltpu.VMEM)] * slots,
        compiler_params=pltpu.CompilerParams(vmem_limit_bytes=40 * MIB),
        cost_estimate=pl.CostEstimate(
            flops=2 * total * depth * width, bytes_accessed=2 * (total * depth + depth * width + total * width), transcendentals=0
        ),
        name="back_parts",
    )(*pieces, weight)


def act_kernel(block, total_rows, *refs):
    pieces = refs[:-3]
    out_ref, whole, *work = refs[-3:]
    damped_moments(pieces, whole, block, total_rows)
    invert_blocks(whole, *work)
    for m in range(whole.shape[0]):
        out_ref[m] = jnp.concatenate(terms(whole[m]), axis=0)


def act_inverses(pieces, block):
    width = pieces[0].shape[1]
    count = width // block
    rows = sum(piece.shape[0] for piece in pieces)
    return pl.pallas_call(
        functools.partial(act_kernel, block, rows),
        out_shape=jax.ShapeDtypeStruct((count, 3 * block, block), jnp.bfloat16),
        in_specs=[pl.BlockSpec(memory_space=pltpu.VMEM)] * len(pieces),
        out_specs=pl.BlockSpec(memory_space=pltpu.VMEM),
        scratch_shapes=scratch_for(count, block),
        compiler_params=pltpu.CompilerParams(vmem_limit_bytes=48 * MIB),
        cost_estimate=pl.CostEstimate(flops=40 * 10**9, bytes_accessed=2 * rows * width, transcendentals=0),
        name="act_inverses",
    )(*pieces)


def update_kernel(total_rows, *refs):
    cot_ref, inverse_ref, *pieces, out_ref = refs
    depth = inverse_ref.shape[2]
    start = 0
    wide = jnp.zeros(out_ref.shape, jnp.float32)
    for piece in pieces:
        length = piece.shape[0]
        wide += jnp.dot(cot_ref[:, start : start + length], piece[...], preferred_element_type=jnp.float32)
        start += length
    a, b, c = terms(wide / total_rows)
    stacked = inverse_ref[0]
    value = jnp.dot(jnp.concatenate([a, a, a], axis=1), stacked, preferred_element_type=jnp.float32)
    value += jnp.dot(jnp.concatenate([b, b], axis=1), stacked[: 2 * depth], preferred_element_type=jnp.float32)
    value += jnp.dot(c, stacked[:depth], preferred_element_type=jnp.float32)
    out_ref[...] = value.astype(jnp.bfloat16)


def update_of(cot_hat, inverses, pieces):
    width = pieces[0].shape[1]
    rows, tokens = cot_hat.shape
    count, depth, block = inverses.shape
    return pl.pallas_call(
        functools.partial(update_kernel, tokens),
        out_shape=jax.ShapeDtypeStruct((rows, width), jnp.bfloat16),
        grid=(count,),
        in_specs=[
            pl.BlockSpec((rows, tokens), lambda m: (0, 0)),
            pl.BlockSpec((1, depth, block), lambda m: (m, 0, 0)),
        ]
        + [pl.BlockSpec((piece.shape[0], block), lambda m: (0, m)) for piece in pieces],
        out_specs=pl.BlockSpec((rows, block), lambda m: (0, m)),
        compiler_params=pltpu.CompilerParams(vmem_limit_bytes=40 * MIB),
        cost_estimate=pl.CostEstimate(flops=6 * 10**9, bytes_accessed=2 * tokens * width, transcendentals=0),
        name="update_tiles",
    )(cot_hat, inverses, *pieces)


def along_x(value, steps):
    pairs = [(z * RING + x, z * RING + (x + steps) % RING) for z in range(2) for x in range(RING)]
    return lax.ppermute(value, "dp", pairs)


def across_z(value):
    return lax.ppermute(value, "dp", [(i, (i + RING) % (2 * RING)) for i in range(2 * RING)])


def section_moves(cross):
    layers, devices = lax.axis_size("section"), 2 * RING
    shift = RING if cross else 0

    def pairs(steps):
        return [(a * devices + i, b * devices + (i + turn) % devices) for a, b, turn in steps for i in range(devices)]

    near = [(a, a - 1, shift) for a in range(1, layers) if a % PLANE]
    far = [(a, a - 1, shift) for a in range(PLANE, layers, PLANE)]
    aside = [(a, a + PLANE - 1, 0) for a in range(PLANE, layers, PLANE)]
    onward = [(a + PLANE - 1, a - 1, shift) for a in range(PLANE, layers, PLANE)]
    return pairs(near + far), pairs(near + aside), pairs(onward)


def handed_first(value, cross):
    split = value.shape[0] * 11 // 16
    direct, beside, _ = section_moves(cross)
    axes = ("section", "dp")
    return lax.ppermute(value[:split], axes, direct), lax.ppermute(value[split:], axes, beside)


def handed_last(direct, beside, cross):
    onward = lax.ppermute(beside, ("section", "dp"), section_moves(cross)[2])
    last = lax.axis_index("section") % PLANE == PLANE - 1
    return jnp.concatenate([direct, jnp.where(last, onward, beside)], axis=0)


def tied(value, after):
    return lax.optimization_barrier((value, after))[0]


def joined(z, mine, other, axis):
    return jnp.where(
        z == 0, jnp.concatenate([mine, other], axis=axis), jnp.concatenate([other, mine], axis=axis)
    )


def shards(activations, cotangents, weights):
    act_tok = activations[0]
    cot_tok = cotangents[0]
    weight_rows = weights[0]
    place = lax.axis_index("dp")
    z, x = place // RING, place % RING
    local_rows, features = act_tok.shape
    block = features // (2 * RING)
    half = features // 2

    def columns(value, start, width):
        return lax.dynamic_slice_in_dim(value, start, width, 1)

    act_theirs = across_z(columns(act_tok, (1 - z) * half, half))

    def cot_for(target):
        return jnp.concatenate(
            [columns(cot_tok, target * block, block), columns(cot_tok, (target + RING) * block, block)], axis=1
        )

    cot_slots = [along_x(cot_for((x + k) % RING), k) for k in range(1, RING)]
    weight_send = columns(weight_rows, (1 - z) * half, half)
    act_theirs, weight_send, *cot_slots = lax.optimization_barrier((act_theirs, weight_send, *cot_slots))
    act_own = jnp.concatenate([columns(act_tok, z * half, half), act_theirs], axis=0)
    act_slots = [act_own] + [along_x(act_own, k) for k in range(1, RING)]
    cot_here = jnp.concatenate([cot_for(x)] + cot_slots, axis=0)
    cot_there = across_z(cot_here)
    weight_theirs = across_z(tied(weight_send, cot_there))
    weight_pair = joined(z, columns(weight_rows, z * half, half), weight_theirs, 0)

    places = tuple(
        tuple((k * local_rows, local_rows, (2 * k + other) * local_rows) for k in range(RING)) for other in range(2)
    )
    cot_theirs, cot_mine = cot_whitened(z, (cot_here, cot_there), places, block)

    def summed(part, moved):
        total = part.astype(jnp.float32)
        for value in moved:
            total = total + value.astype(jnp.float32)
        return total.astype(jnp.bfloat16)

    sides = (2, 1, 3)
    parts_there = back_parts([cot_there], tied(weight_pair, cot_theirs), local_rows)
    moved_there = [along_x(parts_there[k], -k) for k in sides]
    parts_here = back_parts([cot_here], tied(weight_pair, parts_there[0]), local_rows)
    inverses = act_inverses([tied(act_slots[0], (cot_theirs, parts_here[0]))] + act_slots[1:], block)
    inverses, parts_here, *moved_there = lax.optimization_barrier((inverses, parts_here, *moved_there))
    moved_here = [along_x(parts_here[k], -k) for k in sides]
    sum_there = summed(parts_there[0], moved_there)
    down_there = handed_first(sum_there, True)

    inverses, sum_there = lax.optimization_barrier((inverses, sum_there))
    theirs = update_of(cot_theirs, inverses, act_slots)
    sent = across_z(theirs)
    cot_mine, *down_there = lax.optimization_barrier((tied(cot_mine, theirs), *down_there))
    kept = update_of(cot_mine, inverses, act_slots)
    kept, *moved_here = lax.optimization_barrier((kept, *moved_here))
    down_here = handed_first(summed(parts_here[0], moved_here), False)
    back_there = handed_last(*down_there, True)
    back_here = handed_last(*down_here, False)
    handed = joined(z, back_here, back_there, 1)
    update = joined(z, kept, sent, 1)
    return (update[None], handed[None])


def solution(mesh):
    placed = P("section", "dp", None)
    return jax.shard_map(
        shards,
        mesh=mesh,
        in_specs=(placed, placed, placed),
        out_specs=(placed, placed),
        check_vma=False,
    )
```

```python
import functools

import jax
import jax.numpy as jnp
from jax import lax
from jax.experimental import pallas as pl
from jax.experimental.pallas import tpu as pltpu
from jax.sharding import PartitionSpec as P

DAMP = 0.1
TILE = 128
GROUP = 8
RING = 4
PLANE = 8
MIB = 1024 * 1024


def terms(value):
    first = value.astype(jnp.bfloat16)
    rest = value - first.astype(jnp.float32)
    second = rest.astype(jnp.bfloat16)
    third = (rest - second.astype(jnp.float32)).astype(jnp.bfloat16)
    return first, second, third


def dot_wide(left, right):
    a, b, c = terms(left)
    x, y, z = terms(right)
    return jnp.dot(
        jnp.concatenate([a, a, a, b, b, c], axis=1),
        jnp.concatenate([x, y, z, x, y, x], axis=0),
        preferred_element_type=jnp.float32,
    )


def panel_rows(head, first):
    near = [jnp.broadcast_to(head[:, :, first + s : first + s + 1], head.shape) for s in range(GROUP)]
    lane = lax.broadcasted_iota(jnp.int32, head.shape, 2)
    row = lax.broadcasted_iota(jnp.int32, head.shape, 1)
    for t in range(GROUP):
        inverse = 1.0 / near[t][:, t : t + 1]
        pivot_row = jnp.where(lane[:, :1] == first + t, inverse, head[:, t : t + 1] * inverse)
        head = jnp.where(row == t, pivot_row, jnp.where(lane == first + t, 0.0, head) - near[t] * pivot_row)
        for s in range(t + 1, GROUP):
            scaled = near[s][:, t : t + 1] * inverse
            near[s] = jnp.where(row == t, scaled, near[s] - near[t] * scaled)
    return head


def applied(rows, after, first):
    width = after.shape[1]
    lane = lax.broadcasted_iota(jnp.int32, rows.shape, 2)
    parts = [
        jnp.broadcast_to(rows[:, :, first + s : first + s + 1], rows.shape) * after[:, s : s + 1] for s in range(width)
    ]
    while len(parts) > 1:
        parts = [p + q for p, q in zip(parts[::2], parts[1::2])]
    return jnp.where((lane >= first) & (lane < first + width), 0.0, rows) - parts[0]


def float_terms(value):
    return [term.astype(jnp.float32) for term in terms(value)]


def rank_update(matrix, before, after, first):
    size, width = matrix.shape[0], before.shape[0]
    lane = lax.broadcasted_iota(jnp.int32, before.shape, 1)
    a, b, c = float_terms(jnp.where(lane < first, -before, before))
    x, y, z = float_terms(after)
    change = lax.dot_general(
        jnp.concatenate([a, a, a, b, b, c], axis=0).astype(jnp.bfloat16),
        jnp.concatenate([x, y, z, x, y, x], axis=0).astype(jnp.bfloat16),
        (((0,), (0,)), ((), ())),
        preferred_element_type=jnp.float32,
    )
    wide_lane = lax.broadcasted_iota(jnp.int32, (size, size), 1)
    kept = jnp.where((wide_lane >= first) & (wide_lane < first + width), 0.0, matrix) - change
    pieces = [kept[:first], after, kept[first + width :]]
    return jnp.concatenate([piece for piece in pieces if piece.shape[0]], axis=0)


def invert_tiles(tile):
    count, size = tile.shape[0], tile.shape[1]
    step = 2 * GROUP
    head = tile[:, :step]
    for first in range(0, size, step):
        top = panel_rows(head[:, :GROUP], first)
        low = panel_rows(applied(head[:, GROUP:], top, first), first + GROUP)
        after = jnp.concatenate([applied(top, low, first + GROUP), low], axis=1)
        before = head
        if first + step < size:
            head = applied(tile[:, first + step : first + 2 * step], after, first)
        for m in range(count):
            tile[m] = rank_update(tile[m], before[m], after[m], first)


def damped_moments(pieces, whole, block, total_rows):
    count = whole.shape[0]
    eye = lax.broadcasted_iota(jnp.int32, (block, block), 0) == lax.broadcasted_iota(
        jnp.int32, (block, block), 1
    )

    def moment_of(m, carry):
        lanes = pl.ds(pl.multiple_of(m * block, TILE), block)
        moment = jnp.zeros((block, block), jnp.float32)
        for piece in pieces:
            part = piece[:, lanes]
            moment += lax.dot_general(part, part, (((0,), (0,)), ((), ())), preferred_element_type=jnp.float32)
        moment = moment / total_rows
        shift = DAMP * jnp.sum(jnp.where(eye, moment, 0.0)) / block
        whole[m] = moment + jnp.where(eye, shift, 0.0)
        return carry

    lax.fori_loop(0, count, moment_of, 0)


def invert_blocks(whole, tile):
    count, block = whole.shape[0], whole.shape[1]
    steps = block // TILE
    for k in range(steps):
        mine = slice(k * TILE, (k + 1) * TILE)
        others = [slice(j * TILE, (j + 1) * TILE) for j in range(steps) if j != k]
        for m in range(count):
            tile[m] = whole[m, mine, mine]
        invert_tiles(tile)
        for m in range(count):
            pivot = tile[m]
            across = jnp.concatenate([whole[m, mine, j] for j in others], axis=1)
            down = jnp.concatenate([whole[m, i, mine] for i in others], axis=0)
            solved = dot_wide(pivot, across)
            left = dot_wide(down, pivot)
            change = dot_wide(down, solved)
            whole[m, mine, mine] = pivot
            for a, i in enumerate(others):
                here = slice(a * TILE, (a + 1) * TILE)
                whole[m, mine, i] = solved[:, here]
                whole[m, i, mine] = -left[here]
                for b, j in enumerate(others):
                    whole[m, i, j] = whole[m, i, j] - change[here, b * TILE : (b + 1) * TILE]


def scratch_for(count, block):
    return [
        pltpu.VMEM((count, block, block), jnp.float32),
        pltpu.VMEM((count, TILE, TILE), jnp.float32),
    ]


def cot_kernel(places, block, total_rows, place_ref, *refs):
    pieces = refs[: len(places)]
    *outs, stacked, whole, tile = refs[len(places) :]
    count = whole.shape[0]
    damped_moments(pieces, whole, block, total_rows)
    invert_blocks(whole, tile)
    for m in range(count):
        stacked[m] = jnp.concatenate(terms(whole[m]), axis=0)
    own = place_ref[0]
    for out_ref, m in zip(outs, (1 - own, own)):
        lanes = pl.ds(pl.multiple_of(m * block, TILE), block)
        for piece, spots in zip(pieces, places):
            for first, length, place in spots:
                part = piece[first : first + length, lanes]
                value = lax.dot_general(
                    stacked[m],
                    jnp.concatenate([part, part, part], axis=1),
                    (((0,), (1,)), ((), ())),
                    preferred_element_type=jnp.float32,
                )
                out_ref[:, place : place + length] = value.astype(jnp.bfloat16)


def cot_whitened(z, pieces, places, block):
    width = pieces[0].shape[1]
    count = width // block
    rows = sum(piece.shape[0] for piece in pieces)
    return pl.pallas_call(
        functools.partial(cot_kernel, places, block, rows),
        out_shape=[jax.ShapeDtypeStruct((block, rows), jnp.bfloat16)] * 2,
        in_specs=[pl.BlockSpec(memory_space=pltpu.SMEM)] + [pl.BlockSpec(memory_space=pltpu.VMEM)] * len(pieces),
        out_specs=[pl.BlockSpec(memory_space=pltpu.VMEM)] * 2,
        scratch_shapes=[pltpu.VMEM((count, 3 * block, block), jnp.bfloat16)] + scratch_for(count, block),
        compiler_params=pltpu.CompilerParams(vmem_limit_bytes=48 * MIB),
        cost_estimate=pl.CostEstimate(flops=30 * 10**9, bytes_accessed=4 * rows * width, transcendentals=0),
        name="cot_whitened",
    )(z[None], *pieces)


def back_kernel(slots, chunk, *refs):
    *pieces, weight_ref = refs[:-slots]
    outs = refs[-slots:]
    rows = outs[0].shape[0]

    def columns_of(i, carry):
        lanes = pl.ds(pl.multiple_of(i * chunk, TILE), chunk)
        weight = weight_ref[:, lanes]
        at = 0
        for piece in pieces:
            value = jnp.dot(piece[...], weight, preferred_element_type=jnp.float32).astype(jnp.bfloat16)
            for first in range(0, piece.shape[0], rows):
                outs[at][:, lanes] = value[first : first + rows]
                at += 1
        return carry

    lax.fori_loop(0, weight_ref.shape[1] // chunk, columns_of, 0)


def back_parts(pieces, weight, rows):
    total = sum(piece.shape[0] for piece in pieces)
    slots = total // rows
    depth, width = weight.shape
    return pl.pallas_call(
        functools.partial(back_kernel, slots, 2 * TILE),
        out_shape=[jax.ShapeDtypeStruct((rows, width), jnp.bfloat16)] * slots,
        in_specs=[pl.BlockSpec(memory_space=pltpu.VMEM)] * (len(pieces) + 1),
        out_specs=[pl.BlockSpec(memory_space=pltpu.VMEM)] * slots,
        compiler_params=pltpu.CompilerParams(vmem_limit_bytes=40 * MIB),
        cost_estimate=pl.CostEstimate(
            flops=2 * total * depth * width, bytes_accessed=2 * (total * depth + depth * width + total * width), transcendentals=0
        ),
        name="back_parts",
    )(*pieces, weight)


def act_kernel(block, total_rows, *refs):
    pieces = refs[:-3]
    out_ref, whole, *work = refs[-3:]
    damped_moments(pieces, whole, block, total_rows)
    invert_blocks(whole, *work)
    for m in range(whole.shape[0]):
        out_ref[m] = jnp.concatenate(terms(whole[m]), axis=0)


def act_inverses(pieces, block):
    width = pieces[0].shape[1]
    count = width // block
    rows = sum(piece.shape[0] for piece in pieces)
    return pl.pallas_call(
        functools.partial(act_kernel, block, rows),
        out_shape=jax.ShapeDtypeStruct((count, 3 * block, block), jnp.bfloat16),
        in_specs=[pl.BlockSpec(memory_space=pltpu.VMEM)] * len(pieces),
        out_specs=pl.BlockSpec(memory_space=pltpu.VMEM),
        scratch_shapes=scratch_for(count, block),
        compiler_params=pltpu.CompilerParams(vmem_limit_bytes=48 * MIB),
        cost_estimate=pl.CostEstimate(flops=40 * 10**9, bytes_accessed=2 * rows * width, transcendentals=0),
        name="act_inverses",
    )(*pieces)


def update_kernel(total_rows, *refs):
    cot_ref, inverse_ref, *pieces, out_ref = refs
    depth = inverse_ref.shape[2]
    start = 0
    wide = jnp.zeros(out_ref.shape, jnp.float32)
    for piece in pieces:
        length = piece.shape[0]
        wide += jnp.dot(cot_ref[:, start : start + length], piece[...], preferred_element_type=jnp.float32)
        start += length
    a, b, c = terms(wide / total_rows)
    stacked = inverse_ref[0]
    value = jnp.dot(jnp.concatenate([a, a, a], axis=1), stacked, preferred_element_type=jnp.float32)
    value += jnp.dot(jnp.concatenate([b, b], axis=1), stacked[: 2 * depth], preferred_element_type=jnp.float32)
    value += jnp.dot(c, stacked[:depth], preferred_element_type=jnp.float32)
    out_ref[...] = value.astype(jnp.bfloat16)


def update_of(cot_hat, inverses, pieces):
    width = pieces[0].shape[1]
    rows, tokens = cot_hat.shape
    count, depth, block = inverses.shape
    return pl.pallas_call(
        functools.partial(update_kernel, tokens),
        out_shape=jax.ShapeDtypeStruct((rows, width), jnp.bfloat16),
        grid=(count,),
        in_specs=[
            pl.BlockSpec((rows, tokens), lambda m: (0, 0)),
            pl.BlockSpec((1, depth, block), lambda m: (m, 0, 0)),
        ]
        + [pl.BlockSpec((piece.shape[0], block), lambda m: (0, m)) for piece in pieces],
        out_specs=pl.BlockSpec((rows, block), lambda m: (0, m)),
        compiler_params=pltpu.CompilerParams(vmem_limit_bytes=40 * MIB),
        cost_estimate=pl.CostEstimate(flops=6 * 10**9, bytes_accessed=2 * tokens * width, transcendentals=0),
        name="update_tiles",
    )(cot_hat, inverses, *pieces)


def along_x(value, steps):
    pairs = [(z * RING + x, z * RING + (x + steps) % RING) for z in range(2) for x in range(RING)]
    return lax.ppermute(value, "dp", pairs)


def across_z(value):
    return lax.ppermute(value, "dp", [(i, (i + RING) % (2 * RING)) for i in range(2 * RING)])


def section_moves(cross):
    layers, devices = lax.axis_size("section"), 2 * RING
    shift = RING if cross else 0

    def pairs(steps):
        return [(a * devices + i, b * devices + (i + turn) % devices) for a, b, turn in steps for i in range(devices)]

    near = [(a, a - 1, shift) for a in range(1, layers) if a % PLANE]
    far = [(a, a - 1, shift) for a in range(PLANE, layers, PLANE)]
    aside = [(a, a + PLANE - 1, 0) for a in range(PLANE, layers, PLANE)]
    onward = [(a + PLANE - 1, a - 1, shift) for a in range(PLANE, layers, PLANE)]
    return pairs(near + far), pairs(near + aside), pairs(onward)


def handed_first(value, cross):
    split = value.shape[0] // 2
    direct, beside, _ = section_moves(cross)
    axes = ("section", "dp")
    return lax.ppermute(value[:split], axes, direct), lax.ppermute(value[split:], axes, beside)


def handed_last(direct, beside, cross):
    onward = lax.ppermute(beside, ("section", "dp"), section_moves(cross)[2])
    last = lax.axis_index("section") % PLANE == PLANE - 1
    return jnp.concatenate([direct, jnp.where(last, onward, beside)], axis=0)


def tied(value, after):
    return lax.optimization_barrier((value, after))[0]


def joined(z, mine, other, axis):
    return jnp.where(
        z == 0, jnp.concatenate([mine, other], axis=axis), jnp.concatenate([other, mine], axis=axis)
    )


def shards(activations, cotangents, weights):
    act_tok = activations[0]
    cot_tok = cotangents[0]
    weight_rows = weights[0]
    place = lax.axis_index("dp")
    z, x = place // RING, place % RING
    local_rows, features = act_tok.shape
    block = features // (2 * RING)
    half = features // 2

    def columns(value, start, width):
        return lax.dynamic_slice_in_dim(value, start, width, 1)

    act_theirs = across_z(columns(act_tok, (1 - z) * half, half))

    def cot_for(target):
        return jnp.concatenate(
            [columns(cot_tok, target * block, block), columns(cot_tok, (target + RING) * block, block)], axis=1
        )

    cot_slots = [along_x(cot_for((x + k) % RING), k) for k in range(1, RING)]
    weight_send = columns(weight_rows, (1 - z) * half, half)
    act_theirs, weight_send, *cot_slots = lax.optimization_barrier((act_theirs, weight_send, *cot_slots))
    act_own = jnp.concatenate([columns(act_tok, z * half, half), act_theirs], axis=0)
    act_slots = [act_own] + [along_x(act_own, k) for k in range(1, RING)]
    cot_here = jnp.concatenate([cot_for(x)] + cot_slots, axis=0)
    cot_there = across_z(cot_here)
    weight_theirs = across_z(tied(weight_send, cot_there))
    weight_pair = joined(z, columns(weight_rows, z * half, half), weight_theirs, 0)

    places = tuple(
        tuple((k * local_rows, local_rows, (2 * k + other) * local_rows) for k in range(RING)) for other in range(2)
    )
    cot_theirs, cot_mine = cot_whitened(z, (cot_here, cot_there), places, block)

    def summed(part, moved):
        total = part.astype(jnp.float32)
        for value in moved:
            total = total + value.astype(jnp.float32)
        return total.astype(jnp.bfloat16)

    sides = (2, 1, 3)
    parts_there = back_parts([cot_there], tied(weight_pair, cot_theirs), local_rows)
    moved_there = [along_x(parts_there[k], -k) for k in sides]
    parts_here = back_parts([cot_here], tied(weight_pair, parts_there[0]), local_rows)
    inverses = act_inverses([tied(act_slots[0], (cot_theirs, parts_here[0]))] + act_slots[1:], block)
    inverses, parts_here, *moved_there = lax.optimization_barrier((inverses, parts_here, *moved_there))
    moved_here = [along_x(parts_here[k], -k) for k in sides]
    sum_there = summed(parts_there[0], moved_there)
    back_there = lax.ppermute(sum_there, ("section", "dp"), section_moves(True)[0])

    inverses, sum_there = lax.optimization_barrier((inverses, sum_there))
    theirs = update_of(cot_theirs, inverses, act_slots)
    sent = across_z(theirs)
    cot_mine, back_there = lax.optimization_barrier((tied(cot_mine, theirs), back_there))
    kept = update_of(cot_mine, inverses, act_slots)
    kept, *moved_here = lax.optimization_barrier((kept, *moved_here))
    down_here = handed_first(summed(parts_here[0], moved_here), False)
    back_here = handed_last(*down_here, False)
    handed = joined(z, back_here, back_there, 1)
    update = joined(z, kept, sent, 1)
    return (update[None], handed[None])


def solution(mesh):
    placed = P("section", "dp", None)
    return jax.shard_map(
        shards,
        mesh=mesh,
        in_specs=(placed, placed, placed),
        out_specs=(placed, placed),
        check_vma=False,
    )
```
